32 devices in a mesh: grp: 2 (over y), seq: 4 (over z), head: 2 (over x), sub: 2 (over core).
Axes of the slice: x: 2, y: 2, z: 4, core: 2. Of those that a mesh axis runs over, the one named last changes fastest.
Arguments:
- q_mant: bfloat16 [1024, 6144], P(('grp', 'seq', 'head', 'sub')), parts along dimension 0, may hold values from -4 to 4
- q_exp: int32 [1024, 48], P(('grp', 'seq', 'head', 'sub')), parts along dimension 0, may hold values from -2 to 1
- text_kv: bfloat16 [2, 1024, 6144], P(None, 'grp', ('head', 'sub')), parts along dimension 1, may hold values from -4 to 4
- out_weight: bfloat16 [6144, 6144], P(('head', 'sub'), 'seq'), may hold values from -0.3125 to 0.3125
- lengths: int32 [8], P('grp'), parts along dimension 0, may hold values from 64 to 512, as said below
Outputs:
- mixed: bfloat16 [1024, 6144], P(('grp', 'seq', 'head', 'sub')), parts along dimension 0
The draws below stay inside these ranges and needn't reach their ends.
There are 2 independent parts, one for each index of `grp`. The reference program is written for one: setup_inputs(seed, part) draws one part's arguments, and reference() takes and returns one part's arrays. A program takes and returns all parts, laid end to end along the dimension named above; an argument that names none is the same for every part. Nothing has to cross between parts.
Inputs may be any that keep to these rules, and one draw needn't show every extreme that they name: `lengths`: some frame sees all 512 text tokens.
All inputs are finite; a program needn't handle non-finite values.
Results may differ from the reference program's by a relative error of at most 0.009.
Values may be sent and summed in bfloat16 or wider, within the bound.
A program may use at most 128 MiB of HBM per device.

```python
import jax
import jax.numpy as jnp
from jax import lax

H = 48
DH = 128
D = 6144
TXT = 512
FRAME_TOK = 128
TOKENS = 512
FRAMES = 4
N_HEAD = 2
N_SUB = 2


def draw_q_mant(key, part):
    key = jax.random.fold_in(key, 11)
    base = jnp.clip(jax.random.normal(key, (TOKENS, D), jnp.float32), -4.0, 4.0)
    return base.astype(jnp.bfloat16)


def draw_text_kv(key, part):
    key = jax.random.fold_in(key, 23)
    base = jnp.clip(jax.random.normal(key, (2, TXT, D), jnp.float32), -4.0, 4.0)
    return base.astype(jnp.bfloat16)


def draw_lengths(key, part):
    key = jax.random.fold_in(key, 37)
    first, second = jax.random.split(key)
    counts = jax.random.randint(first, (FRAMES,), TXT // 8, TXT + 1)
    chosen = jax.random.randint(second, (), 0, FRAMES)
    return jnp.where(jnp.arange(FRAMES) == chosen, TXT, counts).astype(jnp.int32)


def set_ends(values, own_key, least, high):
    longest = values.shape.index(max(values.shape))
    spots = []
    for shift in (0, 1):
        where = [jax.random.randint(jax.random.fold_in(own_key, axis), (), 0, length) for axis, length in enumerate(values.shape)]
        where[longest] = (where[longest] + shift) % values.shape[longest]
        spots.append(tuple(where))
    return values.at[spots[0]].set(least).at[spots[1]].set(high)


def block_levels(rng, extent, pieces, low, top_value):
    level, own = 1.0, jax.random.fold_in(rng, 6)
    for position, parts in pieces:
        heights = jnp.exp(jax.random.uniform(jax.random.fold_in(own, position), (parts,), jnp.float32, low / len(pieces), top_value / len(pieces)))
        level = level * jnp.repeat(heights, extent[position] // parts).reshape([-1 if axis == position else 1 for axis in range(len(extent))])
    return level


def gaussian(own_key, extent, deviation, most, pieces=(), dtype=jnp.bfloat16):
    loudness = block_levels(own_key, extent, pieces, -0.22, 0.18) if pieces else 1.0
    result = jax.random.normal(own_key, extent, jnp.float32) * deviation * loudness
    return jnp.minimum(jnp.maximum(result, -most), most).astype(dtype)


def setup_inputs(seed: int = 0, part: int = 0) -> dict:
    arg_keys = jax.random.split(jax.random.key(seed), 6)
    part_keys = jax.random.split(jax.random.fold_in(arg_keys[5], part), 6)
    q_mant = draw_q_mant(jax.random.fold_in(jax.random.fold_in(arg_keys[5], part), 71), part)
    q_exp = set_ends(jax.random.randint(part_keys[1], (TOKENS, H), -2, 2), jax.random.fold_in(part_keys[1], 1), -2, 1).astype(jnp.int32)
    text_kv = draw_text_kv(jax.random.fold_in(jax.random.fold_in(arg_keys[5], part), 71), part)
    out_weight = gaussian(arg_keys[3], (D, D), (D // 16) ** -0.5, 0.3125, ((0, 4), (1, 4)))
    lengths = draw_lengths(jax.random.fold_in(jax.random.fold_in(arg_keys[5], part), 71), part)
    return {"q_mant": q_mant, "q_exp": q_exp, "text_kv": text_kv, "out_weight": out_weight, "lengths": lengths}


def reference(q_mant, q_exp, text_kv, out_weight, lengths):
    groups = N_HEAD * N_SUB
    width = (H // groups) * DH
    factor = jnp.exp2(q_exp.astype(jnp.float32))
    query = (q_mant.astype(jnp.float32).reshape(TOKENS, H, DH) * factor[:, :, None]).astype(jnp.bfloat16)
    frame = jnp.arange(TOKENS) // FRAME_TOK
    limit = lengths[frame]
    valid = jnp.arange(TXT)[None, :] < limit[:, None]
    q_heads = jnp.transpose(query, (1, 0, 2))
    k_heads = jnp.transpose(text_kv[0].reshape(TXT, H, DH), (1, 0, 2))
    v_heads = jnp.transpose(text_kv[1].reshape(TXT, H, DH), (1, 0, 2))
    inv = 1.0 / (DH ** 0.5)

    def one_head(items):
        qh, kh, vh = items
        scores = jnp.dot(qh, kh.T, preferred_element_type=jnp.float32) * inv
        scores = jnp.where(valid, scores, -1e30)
        top = jnp.max(scores, axis=1, keepdims=True)
        probs = jnp.where(valid, jnp.exp(scores - top), 0.0)
        total = jnp.sum(probs, axis=1, keepdims=True)
        weights = (probs / total).astype(jnp.bfloat16)
        return jnp.dot(weights, vh, preferred_element_type=jnp.float32).astype(jnp.bfloat16)

    attended = lax.map(one_head, (q_heads, k_heads, v_heads))
    attended = jnp.transpose(attended, (1, 0, 2)).reshape(TOKENS, D)
    summed = jnp.zeros((TOKENS, D), jnp.float32)
    for group in range(groups):
        part = jnp.dot(attended[:, group * width:(group + 1) * width], out_weight[group * width:(group + 1) * width, :], preferred_element_type=jnp.float32)
        part = lax.optimization_barrier(part.astype(jnp.bfloat16))
        summed = summed + part.astype(jnp.float32)
    return summed.astype(jnp.bfloat16)
```

```python
import jax
import jax.numpy as jnp
from jax import lax
from jax.sharding import PartitionSpec as P

FRAME_TOK = 128


def shards(q_mant, q_exp, text_kv, out_weight, lengths):
    tok_dev = q_mant.shape[0]
    heads_all = q_exp.shape[1]
    groups = lax.axis_size("head") * lax.axis_size("sub")
    seq = lax.axis_size("seq")
    local_heads = heads_all // groups
    head_size = q_mant.shape[1] // heads_all
    rows = tok_dev * groups
    factor = jnp.exp2(q_exp.astype(jnp.float32))
    query = (
        q_mant.reshape(tok_dev, heads_all, head_size).astype(jnp.float32) * factor[:, :, None]
    ).astype(jnp.bfloat16)
    query = lax.all_to_all(
        query.reshape(q_mant.shape), ("head", "sub"), split_axis=1, concat_axis=0, tiled=True
    )
    query = query.reshape(rows, local_heads, head_size)
    keys = text_kv[0].reshape(-1, local_heads, head_size)
    values = text_kv[1].reshape(-1, local_heads, head_size)
    text_len = keys.shape[0]
    frames = lengths.shape[0]
    row_index = lax.axis_index("seq") * rows + jnp.arange(rows, dtype=jnp.int32)
    frame = row_index // FRAME_TOK
    limit = jnp.sum(
        jnp.where(
            frame[:, None] == jnp.arange(frames, dtype=jnp.int32)[None, :], lengths[None, :], 0
        ),
        axis=1,
    )
    valid = jnp.arange(text_len, dtype=jnp.int32)[None, :] < limit[:, None]
    scores = jnp.einsum("rhd,thd->hrt", query, keys, preferred_element_type=jnp.float32) * (
        1.0 / head_size**0.5
    )
    scores = jnp.where(valid[None], scores, -1e30)
    top = jnp.max(scores, axis=2, keepdims=True)
    probs = jnp.where(valid[None], jnp.exp(scores - top), 0.0)
    total = jnp.sum(probs, axis=2, keepdims=True)
    weights = (probs / total).astype(jnp.bfloat16)
    attended = jnp.einsum(
        "hrt,thd->rhd", weights, values, preferred_element_type=jnp.float32
    ).astype(jnp.bfloat16)
    attended = attended.reshape(rows, local_heads * head_size)
    gathered = lax.all_gather(attended, "seq", axis=0, tiled=False)
    term = jnp.dot(
        gathered.reshape(seq * rows, -1), out_weight, preferred_element_type=jnp.float32
    ).astype(jnp.bfloat16)
    cols = term.shape[1]
    term = term.reshape(seq, groups, tok_dev, cols).transpose(1, 0, 2, 3)
    summed = lax.psum_scatter(
        term.reshape(groups * seq * tok_dev, cols), ("head", "sub"), scatter_dimension=0, tiled=True
    )
    mixed = lax.all_to_all(
        summed.reshape(seq, tok_dev, cols), "seq", split_axis=0, concat_axis=0, tiled=True
    )
    return mixed.transpose(1, 0, 2).reshape(tok_dev, seq * cols)


def solution(mesh):
    return jax.shard_map(
        shards,
        mesh=mesh,
        in_specs=(
            P(("grp", "seq", "head", "sub"), None),
            P(("grp", "seq", "head", "sub"), None),
            P(None, "grp", ("head", "sub")),
            P(("head", "sub"), "seq"),
            P("grp"),
        ),
        out_specs=P(("grp", "seq", "head", "sub"), None),
        check_vma=False,
    )
```

```python
import functools
import math

import jax
import jax.numpy as jnp
from jax import lax
from jax.experimental import pallas as pl
from jax.experimental.pallas import tpu as pltpu
from jax.sharding import PartitionSpec as P

FRAME_TOK = 128
MESH = pl.DeviceIdType.MESH
CHUNKS = 2
PARTS = 2
BLOCK = 512
UNROLL = 3


def kernel(
    dims, q_ref, e_ref, len_ref, kv_ref, w_ref, out_ref,
    kv, w, qs, qr, att, part, sib, y, rx, done,
    load_sem, q_send, q_recv, att_send, att_recv, sib_send, sib_recv,
    x_send, x_recv, out_send, out_recv,
):
    seq, n_head, n_sub, heads_all = dims
    groups = n_head * n_sub
    head_size = q_ref.shape[1] // heads_all
    width = w_ref.shape[0]
    cols = w_ref.shape[1]
    local_heads = width // head_size
    text_len = kv_ref.shape[1]
    tok = q_ref.shape[0] // CHUNKS
    rows = groups * tok
    part_width = width // PARTS
    part_heads = local_heads // PARTS
    z, h, u = lax.axis_index("seq"), lax.axis_index("head"), lax.axis_index("sub")
    me = h * n_sub + u
    f32, bf16 = jnp.float32, jnp.bfloat16

    loads = [
        pltpu.make_async_copy(kv_ref.at[0], kv.at[0], load_sem.at[0]),
        pltpu.make_async_copy(kv_ref.at[1], kv.at[1], load_sem.at[1]),
        pltpu.make_async_copy(w_ref, w, load_sem.at[2]),
    ]
    for load in loads:
        load.start()

    def owner_id(step):
        peer = lax.rem(me + step, groups)
        return {"head": peer // n_sub, "sub": lax.rem(peer, n_sub)}

    barrier = pltpu.get_barrier_semaphore()
    for step in range(1, groups):
        pl.semaphore_signal(barrier, inc=1, device_id=owner_id(step), device_id_type=MESH)
    for step in range(1, seq):
        pl.semaphore_signal(
            barrier, inc=1, device_id={"seq": lax.rem(z + step, seq)}, device_id_type=MESH
        )

    factor = jnp.exp2(e_ref[...].astype(f32))
    for one in range(heads_all):
        group, local = one // local_heads, one % local_heads
        block = q_ref[:, one * head_size:(one + 1) * head_size].astype(f32)
        block = (block * factor[:, one:one + 1]).astype(bf16)
        for j in range(CHUNKS):
            qs[j, group, :, local * head_size:(local + 1) * head_size] = block[j * tok:(j + 1) * tok]

    pl.semaphore_wait(barrier, groups - 1 + seq - 1)

    def q_copy(j, step):
        return pltpu.make_async_remote_copy(
            src_ref=qs.at[j, lax.rem(me + step, groups)],
            dst_ref=qr.at[j, me],
            send_sem=q_send.at[j, step],
            recv_sem=q_recv.at[j, step],
            device_id=owner_id(step),
            device_id_type=MESH,
        )

    for j in range(CHUNKS):
        for step in range(1, groups):
            q_copy(j, step).start()
    for j in range(CHUNKS):
        qr[j, me] = qs[j, me]

    def att_copy(way, k, t):
        block = z - t if way == 0 else z + t
        place = att.at[k, jnp.clip(block, 0, seq - 1)]
        return pltpu.make_async_remote_copy(
            src_ref=place,
            dst_ref=place,
            send_sem=att_send.at[way, k, t],
            recv_sem=att_recv.at[way, k, t],
            device_id={"seq": z + 1 if way == 0 else z - 1},
            device_id_type=MESH,
        )

    def can_send(way, t):
        return (z - t >= 0) & (z + 1 < seq) if way == 0 else (z + t < seq) & (z - 1 >= 0)

    def can_take(way, t):
        return z - t >= 0 if way == 0 else z + t < seq

    def arrive(k, t):
        for way in range(2):

            @pl.when(can_take(way, t))
            def _():
                block = z - t if way == 0 else z + t
                place = att.at[k, jnp.clip(block, 0, seq - 1)]
                pltpu.make_async_remote_copy(
                    src_ref=place,
                    dst_ref=place,
                    send_sem=att_send.at[way, k, t - 1],
                    recv_sem=att_recv.at[way, k, t - 1],
                    device_id={"seq": z - 1 if way == 0 else z + 1},
                    device_id_type=MESH,
                ).wait_recv()

            if t < seq - 1:

                @pl.when(can_send(way, t))
                def _():
                    att_copy(way, k, t).start()

    rows_seq = q_ref.shape[0] * groups
    limit = len_ref[(z * rows_seq) // FRAME_TOK]
    valid = lax.broadcasted_iota(jnp.int32, (rows, text_len), 1) < limit
    scale = math.log2(math.e) / head_size**0.5

    def attend(k):
        j, c = k // PARTS, k % PARTS

        def some(i, carry):
            for extra in range(UNROLL):
                inner = pl.multiple_of((i * UNROLL + extra) * head_size, head_size)
                outer = pl.multiple_of(c * part_width + inner, head_size)
                query = qr[j, :, :, pl.ds(outer, head_size)].reshape(rows, head_size)
                keys = kv[0, :, pl.ds(outer, head_size)]
                values = kv[1, :, pl.ds(outer, head_size)]
                scores = lax.dot_general(
                    query, keys, (((1,), (1,)), ((), ())), preferred_element_type=f32
                )
                scores = jnp.where(valid, scores, -1e30)
                top = jnp.max(scores, axis=1, keepdims=True)
                probs = jnp.exp2((scores - top) * scale)
                total = jnp.sum(probs, axis=1, keepdims=True)
                mixed = jnp.dot(probs.astype(bf16), values, preferred_element_type=f32)
                att[k, z, :, pl.ds(inner, head_size)] = (mixed * (1.0 / total)).astype(bf16)
            return carry

        lax.fori_loop(0, part_heads // UNROLL, some, 0)
        for way in range(2):

            @pl.when(can_send(way, 0))
            def _():
                att_copy(way, k, 0).start()

    half = seq // 2

    def first_of(i):
        own = z // half
        return (own if i == 0 else 1 - own) * half

    def sib_copy(j, i):
        place = pl.ds(first_of(i), half)
        return pltpu.make_async_remote_copy(
            src_ref=part.at[j, place, 1 - u],
            dst_ref=sib.at[j, place],
            send_sem=sib_send.at[j, i],
            recv_sem=sib_recv.at[j, i],
            device_id={"sub": 1 - u},
            device_id_type=MESH,
        )

    def project(j, i):
        place = pl.ds(first_of(i), half)

        def block(n, carry):
            lanes = pl.ds(pl.multiple_of(n * BLOCK, BLOCK), BLOCK)
            term = None
            for c in range(PARTS):
                left = att[j * PARTS + c, place].reshape(half * rows, part_width)
                more = jnp.dot(
                    left, w[c * part_width:(c + 1) * part_width, lanes], preferred_element_type=f32
                )
                term = more if term is None else term + more
            term = term.astype(bf16).reshape(half, n_head, n_sub, tok, BLOCK)
            for sub in range(n_sub):
                part[j, place, sub, :, :, lanes] = term[:, :, sub]
            return carry

        lax.fori_loop(0, cols // BLOCK, block, 0)
        sib_copy(j, i).start()

    def x_copy(j, i):
        place = pl.ds(first_of(i), half)
        return pltpu.make_async_remote_copy(
            src_ref=y.at[j, place],
            dst_ref=rx.at[j, place],
            send_sem=x_send.at[j, i],
            recv_sem=x_recv.at[j, i],
            device_id={"head": 1 - h},
            device_id_type=MESH,
        )

    def pair(j, i):
        place = pl.ds(first_of(i), half)
        sib_copy(j, i).wait_recv()
        y[j, place] = (
            part[j, place, u, 1 - h].astype(f32) + sib[j, place, 1 - h].astype(f32)
        ).astype(bf16)
        x_copy(j, i).start()

    lanes_out = pl.ds(pl.multiple_of(z * cols, cols), cols)

    def out_copy(j, target):
        return pltpu.make_async_remote_copy(
            src_ref=done.at[j, target],
            dst_ref=out_ref.at[pl.ds(j * tok, tok), lanes_out],
            send_sem=out_send.at[j, target],
            recv_sem=out_recv.at[j, z],
            device_id={"seq": target},
            device_id_type=MESH,
        )

    def finish(j, i):
        place = pl.ds(first_of(i), half)
        x_copy(j, i).wait_recv()
        done[j, place] = (
            part[j, place, u, h].astype(f32) + sib[j, place, h].astype(f32) + rx[j, place].astype(f32)
        ).astype(bf16)
        for one in range(half):
            target = first_of(i) + one

            @pl.when(target != z)
            def _():
                out_copy(j, target).start()

        if i == 0:
            out_ref[pl.ds(j * tok, tok), lanes_out] = done[j, z]

    loads[0].wait()
    loads[1].wait()

    def q_ready(j):
        for step in range(1, groups):
            q_copy(j, step).wait_recv()

    q_ready(0)
    attend(0)
    attend(1)
    arrive(0, 1)
    q_ready(1)
    attend(2)
    arrive(1, 1)
    arrive(0, 2)
    attend(3)
    arrive(2, 1)
    arrive(1, 2)
    loads[2].wait()
    project(0, 0)
    arrive(3, 1)
    arrive(2, 2)
    arrive(0, 3)
    arrive(1, 3)
    project(0, 1)
    arrive(3, 2)
    pair(0, 0)
    project(1, 0)
    pair(0, 1)
    finish(0, 0)
    pair(1, 0)
    finish(0, 1)
    arrive(2, 3)
    arrive(3, 3)
    project(1, 1)
    finish(1, 0)
    pair(1, 1)
    finish(1, 1)

    for j in range(CHUNKS):
        for source in range(seq):

            @pl.when(source != z)
            def _():
                pltpu.make_async_remote_copy(
                    src_ref=done.at[j, source],
                    dst_ref=out_ref.at[pl.ds(j * tok, tok), source * cols:(source + 1) * cols],
                    send_sem=out_send.at[j, source],
                    recv_sem=out_recv.at[j, source],
                    device_id={"seq": source},
                    device_id_type=MESH,
                ).wait_recv()
                out_copy(j, source).wait_send()

        for step in range(1, groups):
            q_copy(j, step).wait_send()
        for i in range(2):
            sib_copy(j, i).wait_send()
            x_copy(j, i).wait_send()
    for way in range(2):
        for k in range(CHUNKS * PARTS):
            for t in range(seq - 1):

                @pl.when(can_send(way, t))
                def _():
                    att_copy(way, k, t).wait_send()


def fused(mesh, q_mant, q_exp, text_kv, out_weight, lengths):
    seq, n_head, n_sub = mesh.shape["seq"], mesh.shape["head"], mesh.shape["sub"]
    groups = n_head * n_sub
    tok = q_mant.shape[0] // CHUNKS
    width, cols = out_weight.shape
    items = CHUNKS * PARTS
    bf16 = jnp.bfloat16
    dma = pltpu.SemaphoreType.DMA
    return pl.pallas_call(
        functools.partial(kernel, (seq, n_head, n_sub, q_exp.shape[1])),
        out_shape=jax.ShapeDtypeStruct(q_mant.shape, bf16),
        in_specs=[
            pl.BlockSpec(memory_space=pltpu.VMEM),
            pl.BlockSpec(memory_space=pltpu.VMEM),
            pl.BlockSpec(memory_space=pltpu.SMEM),
            pl.BlockSpec(memory_space=pl.ANY),
            pl.BlockSpec(memory_space=pl.ANY),
        ],
        out_specs=pl.BlockSpec(memory_space=pltpu.VMEM),
        scratch_shapes=[
            pltpu.VMEM(text_kv.shape, bf16),
            pltpu.VMEM(out_weight.shape, bf16),
            pltpu.VMEM((CHUNKS, groups, tok, width), bf16),
            pltpu.VMEM((CHUNKS, groups, tok, width), bf16),
            pltpu.VMEM((items, seq, groups * tok, width // PARTS), bf16),
            pltpu.VMEM((CHUNKS, seq, n_sub, n_head, tok, cols), bf16),
            pltpu.VMEM((CHUNKS, seq, n_head, tok, cols), bf16),
            pltpu.VMEM((CHUNKS, seq, tok, cols), bf16),
            pltpu.VMEM((CHUNKS, seq, tok, cols), bf16),
            pltpu.VMEM((CHUNKS, seq, tok, cols), bf16),
            dma((3,)),
            dma((CHUNKS, groups)),
            dma((CHUNKS, groups)),
            dma((2, items, seq)),
            dma((2, items, seq)),
            dma((CHUNKS, 2)),
            dma((CHUNKS, 2)),
            dma((CHUNKS, 2)),
            dma((CHUNKS, 2)),
            dma((CHUNKS, seq)),
            dma((CHUNKS, seq)),
        ],
        compiler_params=pltpu.CompilerParams(
            collective_id=0, has_side_effects=True, vmem_limit_bytes=56 * 2**20
        ),
    )(q_mant, q_exp, lengths, text_kv, out_weight)


def fits(mesh, q_mant, q_exp, text_kv, out_weight, lengths):
    if (mesh.shape["seq"], mesh.shape["head"], mesh.shape["sub"]) != (4, 2, 2):
        return False
    head_size = q_mant.shape[1] // q_exp.shape[1]
    return (
        head_size == 128
        and q_mant.shape[0] * 4 == FRAME_TOK
        and q_mant.shape[0] % (16 * CHUNKS) == 0
        and (out_weight.shape[0] // head_size) % (PARTS * UNROLL) == 0
        and out_weight.shape[1] % BLOCK == 0
    )


def shards(q_mant, q_exp, text_kv, out_weight, lengths):
    tok_dev = q_mant.shape[0]
    heads_all = q_exp.shape[1]
    groups = lax.axis_size("head") * lax.axis_size("sub")
    seq = lax.axis_size("seq")
    local_heads = heads_all // groups
    head_size = q_mant.shape[1] // heads_all
    rows = tok_dev * groups
    factor = jnp.exp2(q_exp.astype(jnp.float32))
    query = (
        q_mant.reshape(tok_dev, heads_all, head_size).astype(jnp.float32) * factor[:, :, None]
    ).astype(jnp.bfloat16)
    query = lax.all_to_all(
        query.reshape(q_mant.shape), ("head", "sub"), split_axis=1, concat_axis=0, tiled=True
    )
    query = query.reshape(rows, local_heads, head_size)
    keys = text_kv[0].reshape(-1, local_heads, head_size)
    values = text_kv[1].reshape(-1, local_heads, head_size)
    text_len = keys.shape[0]
    frames = lengths.shape[0]
    row_index = lax.axis_index("seq") * rows + jnp.arange(rows, dtype=jnp.int32)
    frame = row_index // FRAME_TOK
    limit = jnp.sum(
        jnp.where(
            frame[:, None] == jnp.arange(frames, dtype=jnp.int32)[None, :], lengths[None, :], 0
        ),
        axis=1,
    )
    valid = jnp.arange(text_len, dtype=jnp.int32)[None, :] < limit[:, None]
    scores = jnp.einsum("rhd,thd->hrt", query, keys, preferred_element_type=jnp.float32) * (
        1.0 / head_size**0.5
    )
    scores = jnp.where(valid[None], scores, -1e30)
    top = jnp.max(scores, axis=2, keepdims=True)
    probs = jnp.where(valid[None], jnp.exp(scores - top), 0.0)
    total = jnp.sum(probs, axis=2, keepdims=True)
    weights = (probs / total).astype(jnp.bfloat16)
    attended = jnp.einsum(
        "hrt,thd->rhd", weights, values, preferred_element_type=jnp.float32
    ).astype(jnp.bfloat16)
    attended = attended.reshape(rows, local_heads * head_size)
    gathered = lax.all_gather(attended, "seq", axis=0, tiled=False)
    term = jnp.dot(
        gathered.reshape(seq * rows, -1), out_weight, preferred_element_type=jnp.float32
    ).astype(jnp.bfloat16)
    cols = term.shape[1]
    term = term.reshape(seq, groups, tok_dev, cols).transpose(1, 0, 2, 3)
    summed = lax.psum_scatter(
        term.reshape(groups * seq * tok_dev, cols), ("head", "sub"), scatter_dimension=0, tiled=True
    )
    mixed = lax.all_to_all(
        summed.reshape(seq, tok_dev, cols), "seq", split_axis=0, concat_axis=0, tiled=True
    )
    return mixed.transpose(1, 0, 2).reshape(tok_dev, seq * cols)


def solution(mesh):
    def step(*arrays):
        return fused(mesh, *arrays) if fits(mesh, *arrays) else shards(*arrays)

    return jax.shard_map(
        step,
        mesh=mesh,
        in_specs=(
            P(("grp", "seq", "head", "sub"), None),
            P(("grp", "seq", "head", "sub"), None),
            P(None, "grp", ("head", "sub")),
            P(("head", "sub"), "seq"),
            P("grp"),
        ),
        out_specs=P(("grp", "seq", "head", "sub"), None),
        check_vma=False,
    )
```

```python
import functools
import math

import jax
import jax.numpy as jnp
from jax import lax
from jax.experimental import pallas as pl
from jax.experimental.pallas import tpu as pltpu
from jax.sharding import PartitionSpec as P

FRAME_TOK = 128
MESH = pl.DeviceIdType.MESH
BLOCK = 512
UNROLL = 4


def kernel(
    dims, q_ref, e_ref, len_ref, kv_ref, w_ref, out_ref,
    kv, w, qs, qr, att, part, sib, y, rx, done,
    load_sem, q_send, q_recv, att_send, att_recv, sib_send, sib_recv,
    x_send, x_recv, out_send, out_recv,
):
    seq, n_head, n_sub, heads_all = dims
    groups = n_head * n_sub
    head_size = q_ref.shape[1] // heads_all
    width, cols = w_ref.shape
    local_heads = width // head_size
    text_len = kv_ref.shape[1]
    rows = q_ref.shape[0]
    z, h, u = lax.axis_index("seq"), lax.axis_index("head"), lax.axis_index("sub")
    me = h * n_sub + u
    f32, bf16 = jnp.float32, jnp.bfloat16

    loads = [
        pltpu.make_async_copy(kv_ref.at[0], kv.at[0], load_sem.at[0]),
        pltpu.make_async_copy(kv_ref.at[1], kv.at[1], load_sem.at[1]),
        pltpu.make_async_copy(w_ref, w, load_sem.at[2]),
    ]
    for load in loads:
        load.start()

    def owner(d):
        return (h if d < 2 else 1 - h), (u if d % 2 == 0 else 1 - u)

    def owner_id(d):
        head, sub = owner(d)
        return {"head": head, "sub": sub}

    barrier = pltpu.get_barrier_semaphore()
    for d in range(1, groups):
        pl.semaphore_signal(barrier, inc=1, device_id=owner_id(d), device_id_type=MESH)
    for step in range(1, seq):
        pl.semaphore_signal(
            barrier, inc=1, device_id={"seq": lax.rem(z + step, seq)}, device_id_type=MESH
        )

    factor = jnp.exp2(e_ref[...].astype(f32))
    for one in range(heads_all):
        group, local = one // local_heads, one % local_heads
        block = q_ref[:, one * head_size:(one + 1) * head_size].astype(f32)
        block = (block * factor[:, one:one + 1]).astype(bf16)
        qs[group, :, local * head_size:(local + 1) * head_size] = block

    pl.semaphore_wait(barrier, groups - 1 + seq - 1)

    def q_copy(d):
        head, sub = owner(d)
        return pltpu.make_async_remote_copy(
            src_ref=qs.at[head * n_sub + sub],
            dst_ref=qr.at[d],
            send_sem=q_send.at[d],
            recv_sem=q_recv.at[d],
            device_id=owner_id(d),
            device_id_type=MESH,
        )

    for d in (2, 3, 1):
        q_copy(d).start()
    qr[0] = qs[me]

    def block_of(way, t):
        return jnp.clip(z - t if way == 0 else z + t, 0, seq - 1)

    def att_copy(way, t, d, target):
        place = att.at[block_of(way, t), d]
        sem = t if target else t - 1
        return pltpu.make_async_remote_copy(
            src_ref=place,
            dst_ref=place,
            send_sem=att_send.at[way, sem, d],
            recv_sem=att_recv.at[way, sem, d],
            device_id={"seq": z + 1 if (way == 0) == target else z - 1},
            device_id_type=MESH,
        )

    def can_send(way, t):
        return (z - t >= 0) & (z + 1 < seq) if way == 0 else (z + t < seq) & (z - 1 >= 0)

    def can_take(way, t):
        return z - t >= 0 if way == 0 else z + t < seq

    def arrive(t, d):
        for way in range(2):

            @pl.when(can_take(way, t))
            def _():
                att_copy(way, t, d, False).wait_recv()

            if t < seq - 1:

                @pl.when(can_send(way, t))
                def _():
                    att_copy(way, t, d, True).start()

    limit = len_ref[(z * rows * groups) // FRAME_TOK]
    valid = lax.broadcasted_iota(jnp.int32, (rows, text_len), 1) < limit
    scale = math.log2(math.e) / head_size**0.5

    def attend(d):
        def some(i, carry):
            for extra in range(UNROLL):
                lanes = pl.ds(pl.multiple_of((i * UNROLL + extra) * head_size, head_size), head_size)
                scores = lax.dot_general(
                    qr[d, :, lanes], kv[0, :, lanes], (((1,), (1,)), ((), ())),
                    preferred_element_type=f32,
                )
                scores = jnp.where(valid, scores, -1e30)
                top = jnp.max(scores, axis=1, keepdims=True)
                probs = jnp.exp2((scores - top) * scale)
                total = jnp.sum(probs, axis=1, keepdims=True)
                mixed = jnp.dot(probs.astype(bf16), kv[1, :, lanes], preferred_element_type=f32)
                att[z, d, :, lanes] = (mixed * (1.0 / total)).astype(bf16)
            return carry

        lax.fori_loop(0, local_heads // UNROLL, some, 0)
        for way in range(2):

            @pl.when(can_send(way, 0))
            def _():
                att_copy(way, 0, d, True).start()

    last = jnp.where(z < 2, 3, 0)
    second = 1 + lax.rem(z, 2)
    order = (z, second, 6 - z - second - last, last)

    def sib_copy(p, far):
        return pltpu.make_async_remote_copy(
            src_ref=part.at[order[p], 2 * far + 1],
            dst_ref=sib.at[order[p], far],
            send_sem=sib_send.at[p, far],
            recv_sem=sib_recv.at[p, far],
            device_id={"sub": 1 - u},
            device_id_type=MESH,
        )

    def project(p, first, count):
        def block(n, carry):
            lanes = pl.ds(pl.multiple_of(n * BLOCK, BLOCK), BLOCK)
            left = att[order[p], first:first + count].reshape(count * rows, width)
            term = jnp.dot(left, w[:, lanes], preferred_element_type=f32)
            part[order[p], first:first + count, :, lanes] = term.astype(bf16).reshape(
                count, rows, BLOCK
            )
            return carry

        lax.fori_loop(0, cols // BLOCK, block, 0)
        if first + count == groups:
            sib_copy(p, 1).start()
        if first == 0:
            sib_copy(p, 0).start()

    def x_copy(p):
        return pltpu.make_async_remote_copy(
            src_ref=y.at[order[p]],
            dst_ref=rx.at[order[p]],
            send_sem=x_send.at[p],
            recv_sem=x_recv.at[p],
            device_id={"head": 1 - h},
            device_id_type=MESH,
        )

    def pair(p):
        place = order[p]
        sib_copy(p, 1).wait_recv()
        y[place] = (part[place, 2].astype(f32) + sib[place, 1].astype(f32)).astype(bf16)
        x_copy(p).start()

    lanes_out = pl.ds(pl.multiple_of(z * cols, cols), cols)

    def out_copy(p):
        return pltpu.make_async_remote_copy(
            src_ref=done.at[order[p]],
            dst_ref=out_ref.at[:, lanes_out],
            send_sem=out_send.at[p],
            recv_sem=out_recv.at[z],
            device_id={"seq": order[p]},
            device_id_type=MESH,
        )

    def finish(p):
        place = order[p]
        sib_copy(p, 0).wait_recv()
        x_copy(p).wait_recv()
        total = part[place, 0].astype(f32) + sib[place, 0].astype(f32) + rx[place].astype(f32)
        if p == 0:
            out_ref[:, lanes_out] = total.astype(bf16)
        else:
            done[place] = total.astype(bf16)
            out_copy(p).start()

    loads[0].wait()
    loads[1].wait()
    attend(0)
    q_copy(1).wait_recv()
    attend(1)
    arrive(1, 0)
    q_copy(2).wait_recv()
    attend(2)
    arrive(1, 1)
    q_copy(3).wait_recv()
    attend(3)
    arrive(1, 2)
    loads[2].wait()
    project(0, 0, 4)
    arrive(1, 3)
    pair(0)
    project(1, 0, 4)
    pair(1)
    for d in (2, 3, 0, 1):
        arrive(2, d)
    finish(1)
    project(2, 0, 4)
    pair(2)
    finish(2)
    arrive(3, 2)
    arrive(3, 3)
    project(3, 2, 2)
    pair(3)
    arrive(3, 0)
    arrive(3, 1)
    project(3, 0, 2)
    finish(0)
    finish(3)

    for source in range(seq):

        @pl.when(source != z)
        def _():
            pltpu.make_async_remote_copy(
                src_ref=done.at[source],
                dst_ref=out_ref.at[:, source * cols:(source + 1) * cols],
                send_sem=out_send.at[0],
                recv_sem=out_recv.at[source],
                device_id={"seq": source},
                device_id_type=MESH,
            ).wait_recv()

    for d in range(1, groups):
        q_copy(d).wait_send()
    for p in range(seq):
        sib_copy(p, 0).wait_send()
        sib_copy(p, 1).wait_send()
        x_copy(p).wait_send()
        if p:
            out_copy(p).wait_send()
    for way in range(2):
        for t in range(seq - 1):
            for d in range(groups):

                @pl.when(can_send(way, t))
                def _():
                    att_copy(way, t, d, True).wait_send()


def fused(mesh, q_mant, q_exp, text_kv, out_weight, lengths):
    seq, n_head, n_sub = mesh.shape["seq"], mesh.shape["head"], mesh.shape["sub"]
    groups = n_head * n_sub
    rows = q_mant.shape[0]
    width, cols = out_weight.shape
    bf16 = jnp.bfloat16
    dma = pltpu.SemaphoreType.DMA
    return pl.pallas_call(
        functools.partial(kernel, (seq, n_head, n_sub, q_exp.shape[1])),
        out_shape=jax.ShapeDtypeStruct(q_mant.shape, bf16),
        in_specs=[
            pl.BlockSpec(memory_space=pltpu.VMEM),
            pl.BlockSpec(memory_space=pltpu.VMEM),
            pl.BlockSpec(memory_space=pltpu.SMEM),
            pl.BlockSpec(memory_space=pl.ANY),
            pl.BlockSpec(memory_space=pl.ANY),
        ],
        out_specs=pl.BlockSpec(memory_space=pltpu.VMEM),
        scratch_shapes=[
            pltpu.VMEM(text_kv.shape, bf16),
            pltpu.VMEM(out_weight.shape, bf16),
            pltpu.VMEM((groups, rows, width), bf16),
            pltpu.VMEM((groups, rows, width), bf16),
            pltpu.VMEM((seq, groups, rows, width), bf16),
            pltpu.VMEM((seq, groups, rows, cols), bf16),
            pltpu.VMEM((seq, n_head, rows, cols), bf16),
            pltpu.VMEM((seq, rows, cols), bf16),
            pltpu.VMEM((seq, rows, cols), bf16),
            pltpu.VMEM((seq, rows, cols), bf16),
            dma((3,)),
            dma((groups,)),
            dma((groups,)),
            dma((2, seq, groups)),
            dma((2, seq, groups)),
            dma((seq, 2)),
            dma((seq, 2)),
            dma((seq,)),
            dma((seq,)),
            dma((seq,)),
            dma((seq,)),
        ],
        compiler_params=pltpu.CompilerParams(
            collective_id=0, has_side_effects=True, vmem_limit_bytes=56 * 2**20
        ),
    )(q_mant, q_exp, lengths, text_kv, out_weight)


def fits(mesh, q_mant, q_exp, text_kv, out_weight, lengths):
    if (mesh.shape["seq"], mesh.shape["head"], mesh.shape["sub"]) != (4, 2, 2):
        return False
    head_size = q_mant.shape[1] // q_exp.shape[1]
    return (
        head_size == 128
        and q_mant.shape[0] * 4 == FRAME_TOK
        and q_mant.shape[0] % 16 == 0
        and (out_weight.shape[0] // head_size) % UNROLL == 0
        and out_weight.shape[1] % BLOCK == 0
    )


def shards(q_mant, q_exp, text_kv, out_weight, lengths):
    tok_dev = q_mant.shape[0]
    heads_all = q_exp.shape[1]
    groups = lax.axis_size("head") * lax.axis_size("sub")
    seq = lax.axis_size("seq")
    local_heads = heads_all // groups
    head_size = q_mant.shape[1] // heads_all
    rows = tok_dev * groups
    factor = jnp.exp2(q_exp.astype(jnp.float32))
    query = (
        q_mant.reshape(tok_dev, heads_all, head_size).astype(jnp.float32) * factor[:, :, None]
    ).astype(jnp.bfloat16)
    query = lax.all_to_all(
        query.reshape(q_mant.shape), ("head", "sub"), split_axis=1, concat_axis=0, tiled=True
    )
    query = query.reshape(rows, local_heads, head_size)
    keys = text_kv[0].reshape(-1, local_heads, head_size)
    values = text_kv[1].reshape(-1, local_heads, head_size)
    text_len = keys.shape[0]
    frames = lengths.shape[0]
    row_index = lax.axis_index("seq") * rows + jnp.arange(rows, dtype=jnp.int32)
    frame = row_index // FRAME_TOK
    limit = jnp.sum(
        jnp.where(
            frame[:, None] == jnp.arange(frames, dtype=jnp.int32)[None, :], lengths[None, :], 0
        ),
        axis=1,
    )
    valid = jnp.arange(text_len, dtype=jnp.int32)[None, :] < limit[:, None]
    scores = jnp.einsum("rhd,thd->hrt", query, keys, preferred_element_type=jnp.float32) * (
        1.0 / head_size**0.5
    )
    scores = jnp.where(valid[None], scores, -1e30)
    top = jnp.max(scores, axis=2, keepdims=True)
    probs = jnp.where(valid[None], jnp.exp(scores - top), 0.0)
    total = jnp.sum(probs, axis=2, keepdims=True)
    weights = (probs / total).astype(jnp.bfloat16)
    attended = jnp.einsum(
        "hrt,thd->rhd", weights, values, preferred_element_type=jnp.float32
    ).astype(jnp.bfloat16)
    attended = attended.reshape(rows, local_heads * head_size)
    gathered = lax.all_gather(attended, "seq", axis=0, tiled=False)
    term = jnp.dot(
        gathered.reshape(seq * rows, -1), out_weight, preferred_element_type=jnp.float32
    ).astype(jnp.bfloat16)
    cols = term.shape[1]
    term = term.reshape(seq, groups, tok_dev, cols).transpose(1, 0, 2, 3)
    summed = lax.psum_scatter(
        term.reshape(groups * seq * tok_dev, cols), ("head", "sub"), scatter_dimension=0, tiled=True
    )
    mixed = lax.all_to_all(
        summed.reshape(seq, tok_dev, cols), "seq", split_axis=0, concat_axis=0, tiled=True
    )
    return mixed.transpose(1, 0, 2).reshape(tok_dev, seq * cols)


def solution(mesh):
    def step(*arrays):
        return fused(mesh, *arrays) if fits(mesh, *arrays) else shards(*arrays)

    return jax.shard_map(
        step,
        mesh=mesh,
        in_specs=(
            P(("grp", "seq", "head", "sub"), None),
            P(("grp", "seq", "head", "sub"), None),
            P(None, "grp", ("head", "sub")),
            P(("head", "sub"), "seq"),
            P("grp"),
        ),
        out_specs=P(("grp", "seq", "head", "sub"), None),
        check_vma=False,
    )
```

```python
import functools
import math

import jax
import jax.numpy as jnp
from jax import lax
from jax.experimental import pallas as pl
from jax.experimental.pallas import tpu as pltpu
from jax.sharding import PartitionSpec as P

FRAME_TOK = 128
MESH = pl.DeviceIdType.MESH
BLOCK = 512
UNROLL = 12


def kernel(
    dims, q_ref, e_ref, len_ref, kv_ref, w_ref, out_ref,
    kv, w, qs, qr, att, part, sib, y, rx, done,
    load_sem, q_send, q_recv, att_send, att_recv, sib_send, sib_recv,
    x_send, x_recv, out_send, out_recv,
):
    seq, n_head, n_sub, heads_all = dims
    groups = n_head * n_sub
    head_size = q_ref.shape[1] // heads_all
    width, cols = w_ref.shape
    local_heads = width // head_size
    text_len = kv_ref.shape[1]
    rows = q_ref.shape[0]
    z, h, u = lax.axis_index("seq"), lax.axis_index("head"), lax.axis_index("sub")
    me = h * n_sub + u
    f32, bf16 = jnp.float32, jnp.bfloat16

    loads = [
        pltpu.make_async_copy(kv_ref.at[0], kv.at[0], load_sem.at[0]),
        pltpu.make_async_copy(kv_ref.at[1], kv.at[1], load_sem.at[1]),
        pltpu.make_async_copy(w_ref, w, load_sem.at[2]),
    ]
    for load in loads:
        load.start()

    def owner(d):
        return (h if d < 2 else 1 - h), (u if d % 2 == 0 else 1 - u)

    def owner_id(d):
        head, sub = owner(d)
        return {"head": head, "sub": sub}

    barrier = pltpu.get_barrier_semaphore()
    for d in range(1, groups):
        pl.semaphore_signal(barrier, inc=1, device_id=owner_id(d), device_id_type=MESH)
    for step in range(1, seq):
        pl.semaphore_signal(
            barrier, inc=1, device_id={"seq": lax.rem(z + step, seq)}, device_id_type=MESH
        )

    factor = jnp.exp2(e_ref[...].astype(f32))
    for one in range(heads_all):
        group, local = one // local_heads, one % local_heads
        block = q_ref[:, one * head_size:(one + 1) * head_size].astype(f32)
        block = (block * factor[:, one:one + 1]).astype(bf16)
        qs[group, :, local * head_size:(local + 1) * head_size] = block

    pl.semaphore_wait(barrier, groups - 1 + seq - 1)

    def q_copy(d):
        head, sub = owner(d)
        return pltpu.make_async_remote_copy(
            src_ref=qs.at[head * n_sub + sub],
            dst_ref=qr.at[d],
            send_sem=q_send.at[d],
            recv_sem=q_recv.at[d],
            device_id=owner_id(d),
            device_id_type=MESH,
        )

    for d in (2, 3, 1):
        q_copy(d).start()
    qr[0] = qs[me]

    def block_of(way, t):
        return jnp.clip(z - t if way == 0 else z + t, 0, seq - 1)

    def att_copy(way, t, d, target):
        place = att.at[block_of(way, t), d]
        sem = t if target else t - 1
        return pltpu.make_async_remote_copy(
            src_ref=place,
            dst_ref=place,
            send_sem=att_send.at[way, sem, d],
            recv_sem=att_recv.at[way, sem, d],
            device_id={"seq": z + 1 if (way == 0) == target else z - 1},
            device_id_type=MESH,
        )

    def can_send(way, t):
        return (z - t >= 0) & (z + 1 < seq) if way == 0 else (z + t < seq) & (z - 1 >= 0)

    def can_take(way, t):
        return z - t >= 0 if way == 0 else z + t < seq

    def arrive(t, d):
        for way in range(2):

            @pl.when(can_take(way, t))
            def _():
                att_copy(way, t, d, False).wait_recv()

            if t < seq - 1:

                @pl.when(can_send(way, t))
                def _():
                    att_copy(way, t, d, True).start()

    limit = len_ref[(z * rows * groups) // FRAME_TOK]
    valid = lax.broadcasted_iota(jnp.int32, (rows, text_len), 1) < limit
    scale = math.log2(math.e) / head_size**0.5

    def attend(d):
        def some(i, carry):
            lanes = [
                pl.ds(pl.multiple_of((i * UNROLL + extra) * head_size, head_size), head_size)
                for extra in range(UNROLL)
            ]
            scores = [
                lax.dot_general(
                    qr[d, :, one], kv[0, :, one], (((1,), (1,)), ((), ())),
                    preferred_element_type=f32,
                )
                for one in lanes
            ]
            scores = [jnp.where(valid, one, -1e30) for one in scores]
            tops = [jnp.max(one, axis=1, keepdims=True) for one in scores]
            probs = [jnp.exp2((one - top) * scale) for one, top in zip(scores, tops)]
            totals = [jnp.sum(one, axis=1, keepdims=True) for one in probs]
            mixed = [
                jnp.dot(prob.astype(bf16), kv[1, :, one], preferred_element_type=f32)
                for prob, one in zip(probs, lanes)
            ]
            for one, value, total in zip(lanes, mixed, totals):
                att[z, d, :, one] = (value * (1.0 / total)).astype(bf16)
            return carry

        lax.fori_loop(0, local_heads // UNROLL, some, 0)
        for way in range(2):

            @pl.when(can_send(way, 0))
            def _():
                att_copy(way, 0, d, True).start()

    last = jnp.where(z < 2, 3, 0)
    second = 1 + lax.rem(z, 2)
    order = (z, second, 6 - z - second - last, last)

    def sib_copy(p, far):
        return pltpu.make_async_remote_copy(
            src_ref=part.at[order[p], 2 * far + 1],
            dst_ref=sib.at[order[p], far],
            send_sem=sib_send.at[p, far],
            recv_sem=sib_recv.at[p, far],
            device_id={"sub": 1 - u},
            device_id_type=MESH,
        )

    def project(p, first, count):
        def block(n, carry):
            lanes = pl.ds(pl.multiple_of(n * BLOCK, BLOCK), BLOCK)
            left = att[order[p], first:first + count].reshape(count * rows, width)
            term = jnp.dot(left, w[:, lanes], preferred_element_type=f32)
            part[order[p], first:first + count, :, lanes] = term.astype(bf16).reshape(
                count, rows, BLOCK
            )
            return carry

        lax.fori_loop(0, cols // BLOCK, block, 0)
        if first + count == groups:
            sib_copy(p, 1).start()
        if first == 0:
            sib_copy(p, 0).start()

    def x_copy(p):
        return pltpu.make_async_remote_copy(
            src_ref=y.at[order[p]],
            dst_ref=rx.at[order[p]],
            send_sem=x_send.at[p],
            recv_sem=x_recv.at[p],
            device_id={"head": 1 - h},
            device_id_type=MESH,
        )

    def pair(p):
        place = order[p]
        sib_copy(p, 1).wait_recv()
        y[place] = (part[place, 2].astype(f32) + sib[place, 1].astype(f32)).astype(bf16)
        x_copy(p).start()

    lanes_out = pl.ds(pl.multiple_of(z * cols, cols), cols)

    def out_copy(p):
        return pltpu.make_async_remote_copy(
            src_ref=done.at[order[p]],
            dst_ref=out_ref.at[:, lanes_out],
            send_sem=out_send.at[p],
            recv_sem=out_recv.at[z],
            device_id={"seq": order[p]},
            device_id_type=MESH,
        )

    def finish(p):
        place = order[p]
        sib_copy(p, 0).wait_recv()
        x_copy(p).wait_recv()
        total = part[place, 0].astype(f32) + sib[place, 0].astype(f32) + rx[place].astype(f32)
        if p == 0:
            out_ref[:, lanes_out] = total.astype(bf16)
        else:
            done[place] = total.astype(bf16)
            out_copy(p).start()

    loads[0].wait()
    loads[1].wait()
    attend(0)
    q_copy(1).wait_recv()
    attend(1)
    arrive(1, 0)
    q_copy(2).wait_recv()
    attend(2)
    arrive(1, 1)
    q_copy(3).wait_recv()
    attend(3)
    arrive(1, 2)
    loads[2].wait()
    project(0, 0, 4)
    arrive(1, 3)
    pair(0)
    project(1, 0, 4)
    pair(1)
    for d in (2, 3, 0, 1):
        arrive(2, d)
    finish(1)
    project(2, 0, 4)
    pair(2)
    finish(2)
    arrive(3, 2)
    arrive(3, 3)
    project(3, 2, 2)
    pair(3)
    arrive(3, 0)
    arrive(3, 1)
    project(3, 0, 2)
    finish(0)
    finish(3)

    for source in range(seq):

        @pl.when(source != z)
        def _():
            pltpu.make_async_remote_copy(
                src_ref=done.at[source],
                dst_ref=out_ref.at[:, source * cols:(source + 1) * cols],
                send_sem=out_send.at[0],
                recv_sem=out_recv.at[source],
                device_id={"seq": source},
                device_id_type=MESH,
            ).wait_recv()

    for d in range(1, groups):
        q_copy(d).wait_send()
    for p in range(seq):
        sib_copy(p, 0).wait_send()
        sib_copy(p, 1).wait_send()
        x_copy(p).wait_send()
        if p:
            out_copy(p).wait_send()
    for way in range(2):
        for t in range(seq - 1):
            for d in range(groups):

                @pl.when(can_send(way, t))
                def _():
                    att_copy(way, t, d, True).wait_send()


def fused(mesh, q_mant, q_exp, text_kv, out_weight, lengths):
    seq, n_head, n_sub = mesh.shape["seq"], mesh.shape["head"], mesh.shape["sub"]
    groups = n_head * n_sub
    rows = q_mant.shape[0]
    width, cols = out_weight.shape
    bf16 = jnp.bfloat16
    dma = pltpu.SemaphoreType.DMA
    return pl.pallas_call(
        functools.partial(kernel, (seq, n_head, n_sub, q_exp.shape[1])),
        out_shape=jax.ShapeDtypeStruct(q_mant.shape, bf16),
        in_specs=[
            pl.BlockSpec(memory_space=pltpu.VMEM),
            pl.BlockSpec(memory_space=pltpu.VMEM),
            pl.BlockSpec(memory_space=pltpu.SMEM),
            pl.BlockSpec(memory_space=pl.ANY),
            pl.BlockSpec(memory_space=pl.ANY),
        ],
        out_specs=pl.BlockSpec(memory_space=pltpu.VMEM),
        scratch_shapes=[
            pltpu.VMEM(text_kv.shape, bf16),
            pltpu.VMEM(out_weight.shape, bf16),
            pltpu.VMEM((groups, rows, width), bf16),
            pltpu.VMEM((groups, rows, width), bf16),
            pltpu.VMEM((seq, groups, rows, width), bf16),
            pltpu.VMEM((seq, groups, rows, cols), bf16),
            pltpu.VMEM((seq, n_head, rows, cols), bf16),
            pltpu.VMEM((seq, rows, cols), bf16),
            pltpu.VMEM((seq, rows, cols), bf16),
            pltpu.VMEM((seq, rows, cols), bf16),
            dma((3,)),
            dma((groups,)),
            dma((groups,)),
            dma((2, seq, groups)),
            dma((2, seq, groups)),
            dma((seq, 2)),
            dma((seq, 2)),
            dma((seq,)),
            dma((seq,)),
            dma((seq,)),
            dma((seq,)),
        ],
        compiler_params=pltpu.CompilerParams(
            collective_id=0, has_side_effects=True, vmem_limit_bytes=56 * 2**20
        ),
    )(q_mant, q_exp, lengths, text_kv, out_weight)


def fits(mesh, q_mant, q_exp, text_kv, out_weight, lengths):
    if (mesh.shape["seq"], mesh.shape["head"], mesh.shape["sub"]) != (4, 2, 2):
        return False
    head_size = q_mant.shape[1] // q_exp.shape[1]
    return (
        head_size == 128
        and q_mant.shape[0] * 4 == FRAME_TOK
        and q_mant.shape[0] % 16 == 0
        and (out_weight.shape[0] // head_size) % UNROLL == 0
        and out_weight.shape[1] % BLOCK == 0
    )


def shards(q_mant, q_exp, text_kv, out_weight, lengths):
    tok_dev = q_mant.shape[0]
    heads_all = q_exp.shape[1]
    groups = lax.axis_size("head") * lax.axis_size("sub")
    seq = lax.axis_size("seq")
    local_heads = heads_all // groups
    head_size = q_mant.shape[1] // heads_all
    rows = tok_dev * groups
    factor = jnp.exp2(q_exp.astype(jnp.float32))
    query = (
        q_mant.reshape(tok_dev, heads_all, head_size).astype(jnp.float32) * factor[:, :, None]
    ).astype(jnp.bfloat16)
    query = lax.all_to_all(
        query.reshape(q_mant.shape), ("head", "sub"), split_axis=1, concat_axis=0, tiled=True
    )
    query = query.reshape(rows, local_heads, head_size)
    keys = text_kv[0].reshape(-1, local_heads, head_size)
    values = text_kv[1].reshape(-1, local_heads, head_size)
    text_len = keys.shape[0]
    frames = lengths.shape[0]
    row_index = lax.axis_index("seq") * rows + jnp.arange(rows, dtype=jnp.int32)
    frame = row_index // FRAME_TOK
    limit = jnp.sum(
        jnp.where(
            frame[:, None] == jnp.arange(frames, dtype=jnp.int32)[None, :], lengths[None, :], 0
        ),
        axis=1,
    )
    valid = jnp.arange(text_len, dtype=jnp.int32)[None, :] < limit[:, None]
    scores = jnp.einsum("rhd,thd->hrt", query, keys, preferred_element_type=jnp.float32) * (
        1.0 / head_size**0.5
    )
    scores = jnp.where(valid[None], scores, -1e30)
    top = jnp.max(scores, axis=2, keepdims=True)
    probs = jnp.where(valid[None], jnp.exp(scores - top), 0.0)
    total = jnp.sum(probs, axis=2, keepdims=True)
    weights = (probs / total).astype(jnp.bfloat16)
    attended = jnp.einsum(
        "hrt,thd->rhd", weights, values, preferred_element_type=jnp.float32
    ).astype(jnp.bfloat16)
    attended = attended.reshape(rows, local_heads * head_size)
    gathered = lax.all_gather(attended, "seq", axis=0, tiled=False)
    term = jnp.dot(
        gathered.reshape(seq * rows, -1), out_weight, preferred_element_type=jnp.float32
    ).astype(jnp.bfloat16)
    cols = term.shape[1]
    term = term.reshape(seq, groups, tok_dev, cols).transpose(1, 0, 2, 3)
    summed = lax.psum_scatter(
        term.reshape(groups * seq * tok_dev, cols), ("head", "sub"), scatter_dimension=0, tiled=True
    )
    mixed = lax.all_to_all(
        summed.reshape(seq, tok_dev, cols), "seq", split_axis=0, concat_axis=0, tiled=True
    )
    return mixed.transpose(1, 0, 2).reshape(tok_dev, seq * cols)


def solution(mesh):
    def step(*arrays):
        return fused(mesh, *arrays) if fits(mesh, *arrays) else shards(*arrays)

    return jax.shard_map(
        step,
        mesh=mesh,
        in_specs=(
            P(("grp", "seq", "head", "sub"), None),
            P(("grp", "seq", "head", "sub"), None),
            P(None, "grp", ("head", "sub")),
            P(("head", "sub"), "seq"),
            P("grp"),
        ),
        out_specs=P(("grp", "seq", "head", "sub"), None),
        check_vma=False,
    )
```

```python
import functools
import math

import jax
import jax.numpy as jnp
from jax import lax
from jax.experimental import pallas as pl
from jax.experimental.pallas import tpu as pltpu
from jax.sharding import PartitionSpec as P

FRAME_TOK = 128
MESH = pl.DeviceIdType.MESH
BLOCK = 512
UNROLL = 12


def kernel(
    dims, q_ref, e_ref, len_ref, kv_ref, w_ref, out_ref,
    kv, w, qs, qr, att, part, sib, y, rx, done,
    load_sem, q_send, q_recv, att_send, att_recv, sib_send, sib_recv,
    x_send, x_recv, out_send, out_recv,
):
    seq, n_head, n_sub, heads_all = dims
    groups = n_head * n_sub
    head_size = q_ref.shape[1] // heads_all
    width, cols = w_ref.shape
    local_heads = width // head_size
    text_len = kv_ref.shape[1]
    rows = q_ref.shape[0]
    z, h, u = lax.axis_index("seq"), lax.axis_index("head"), lax.axis_index("sub")
    me = h * n_sub + u
    f32, bf16 = jnp.float32, jnp.bfloat16

    loads = [
        pltpu.make_async_copy(kv_ref.at[0], kv.at[0], load_sem.at[0]),
        pltpu.make_async_copy(kv_ref.at[1], kv.at[1], load_sem.at[1]),
        pltpu.make_async_copy(w_ref, w, load_sem.at[2]),
    ]
    for load in loads:
        load.start()

    def owner(d):
        return (h if d < 2 else 1 - h), (u if d % 2 == 0 else 1 - u)

    def owner_id(d):
        head, sub = owner(d)
        return {"head": head, "sub": sub}

    barrier = pltpu.get_barrier_semaphore()
    for d in range(1, groups):
        pl.semaphore_signal(barrier, inc=1, device_id=owner_id(d), device_id_type=MESH)
    for step in range(1, seq):
        pl.semaphore_signal(
            barrier, inc=1, device_id={"seq": lax.rem(z + step, seq)}, device_id_type=MESH
        )

    factor = jnp.exp2(e_ref[...].astype(f32))
    for one in range(heads_all):
        group, local = one // local_heads, one % local_heads
        block = q_ref[:, one * head_size:(one + 1) * head_size].astype(f32)
        block = (block * factor[:, one:one + 1]).astype(bf16)
        qs[group, :, local * head_size:(local + 1) * head_size] = block

    pl.semaphore_wait(barrier, groups - 1 + seq - 1)

    def q_copy(d):
        head, sub = owner(d)
        return pltpu.make_async_remote_copy(
            src_ref=qs.at[head * n_sub + sub],
            dst_ref=qr.at[d],
            send_sem=q_send.at[d],
            recv_sem=q_recv.at[d],
            device_id=owner_id(d),
            device_id_type=MESH,
        )

    for d in (2, 3, 1):
        q_copy(d).start()
    qr[0] = qs[me]

    def block_of(way, t):
        return jnp.clip(z - t if way == 0 else z + t, 0, seq - 1)

    def att_copy(way, t, d, target):
        place = att.at[block_of(way, t), d]
        sem = t if target else t - 1
        return pltpu.make_async_remote_copy(
            src_ref=place,
            dst_ref=place,
            send_sem=att_send.at[way, sem, d],
            recv_sem=att_recv.at[way, sem, d],
            device_id={"seq": z + 1 if (way == 0) == target else z - 1},
            device_id_type=MESH,
        )

    def can_send(way, t):
        return (z - t >= 0) & (z + 1 < seq) if way == 0 else (z + t < seq) & (z - 1 >= 0)

    def can_take(way, t):
        return z - t >= 0 if way == 0 else z + t < seq

    def arrive(t, d):
        for way in range(2):

            @pl.when(can_take(way, t))
            def _():
                att_copy(way, t, d, False).wait_recv()

            if t < seq - 1:

                @pl.when(can_send(way, t))
                def _():
                    att_copy(way, t, d, True).start()

    limit = len_ref[(z * rows * groups) // FRAME_TOK]
    valid = lax.broadcasted_iota(jnp.int32, (rows, text_len), 1) < limit
    scale = math.log2(math.e) / head_size**0.5

    def attend(d):
        def some(i, carry):
            lanes = [
                pl.ds(pl.multiple_of((i * UNROLL + extra) * head_size, head_size), head_size)
                for extra in range(UNROLL)
            ]
            scores = [
                lax.dot_general(
                    qr[d, :, one], kv[0, :, one], (((1,), (1,)), ((), ())),
                    preferred_element_type=f32,
                )
                for one in lanes
            ]
            scores = [jnp.where(valid, one, -1e30) for one in scores]
            tops = [jnp.max(one, axis=1, keepdims=True) for one in scores]
            probs = [jnp.exp2((one - top) * scale) for one, top in zip(scores, tops)]
            totals = [jnp.sum(one, axis=1, keepdims=True) for one in probs]
            mixed = [
                jnp.dot(prob.astype(bf16), kv[1, :, one], preferred_element_type=f32)
                for prob, one in zip(probs, lanes)
            ]
            for one, value, total in zip(lanes, mixed, totals):
                att[z, d, :, one] = (value * (1.0 / total)).astype(bf16)
            return carry

        lax.fori_loop(0, local_heads // UNROLL, some, 0)
        for way in range(2):

            @pl.when(can_send(way, 0))
            def _():
                att_copy(way, 0, d, True).start()

    last = jnp.where(z < 2, 3, 0)
    second = 1 + lax.rem(z, 2)
    order = (z, second, 6 - z - second - last, last)

    def sib_copy(p, far):
        return pltpu.make_async_remote_copy(
            src_ref=part.at[order[p], 2 * far + 1],
            dst_ref=sib.at[order[p], far],
            send_sem=sib_send.at[p, far],
            recv_sem=sib_recv.at[p, far],
            device_id={"sub": 1 - u},
            device_id_type=MESH,
        )

    def project(p, first, count):
        def block(n, carry):
            lanes = pl.ds(pl.multiple_of(n * BLOCK, BLOCK), BLOCK)
            left = att[order[p], first:first + count].reshape(count * rows, width)
            term = jnp.dot(left, w[:, lanes], preferred_element_type=f32)
            part[order[p], first:first + count, :, lanes] = term.astype(bf16).reshape(
                count, rows, BLOCK
            )
            return carry

        lax.fori_loop(0, cols // BLOCK, block, 0)
        if first + count == groups:
            sib_copy(p, 1).start()
        if first == 0:
            sib_copy(p, 0).start()

    def x_copy(p):
        return pltpu.make_async_remote_copy(
            src_ref=y.at[order[p]],
            dst_ref=rx.at[order[p]],
            send_sem=x_send.at[p],
            recv_sem=x_recv.at[p],
            device_id={"head": 1 - h},
            device_id_type=MESH,
        )

    def pair(p):
        place = order[p]
        sib_copy(p, 1).wait_recv()
        y[place] = (part[place, 2].astype(f32) + sib[place, 1].astype(f32)).astype(bf16)
        x_copy(p).start()

    lanes_out = pl.ds(pl.multiple_of(z * cols, cols), cols)

    def out_copy(p):
        return pltpu.make_async_remote_copy(
            src_ref=done.at[order[p]],
            dst_ref=out_ref.at[:, lanes_out],
            send_sem=out_send.at[p],
            recv_sem=out_recv.at[z],
            device_id={"seq": order[p]},
            device_id_type=MESH,
        )

    def finish(p):
        place = order[p]
        sib_copy(p, 0).wait_recv()
        x_copy(p).wait_recv()
        total = part[place, 0].astype(f32) + sib[place, 0].astype(f32) + rx[place].astype(f32)
        if p == 0:
            out_ref[:, lanes_out] = total.astype(bf16)
        else:
            done[place] = total.astype(bf16)
            out_copy(p).start()

    loads[0].wait()
    loads[1].wait()
    attend(0)
    q_copy(1).wait_recv()
    attend(1)
    arrive(1, 0)
    q_copy(2).wait_recv()
    attend(2)
    arrive(1, 1)
    q_copy(3).wait_recv()
    attend(3)
    arrive(1, 2)
    loads[2].wait()
    project(0, 0, 4)
    arrive(1, 3)
    pair(0)
    project(1, 0, 4)
    pair(1)
    for d in (2, 3, 0, 1):
        arrive(2, d)
    project(2, 0, 4)
    pair(2)
    arrive(3, 2)
    arrive(3, 3)
    project(3, 2, 2)
    pair(3)
    finish(1)
    finish(2)
    arrive(3, 0)
    arrive(3, 1)
    project(3, 0, 2)
    finish(3)
    finish(0)

    for source in range(seq):

        @pl.when(source != z)
        def _():
            pltpu.make_async_remote_copy(
                src_ref=done.at[source],
                dst_ref=out_ref.at[:, source * cols:(source + 1) * cols],
                send_sem=out_send.at[0],
                recv_sem=out_recv.at[source],
                device_id={"seq": source},
                device_id_type=MESH,
            ).wait_recv()

    for d in range(1, groups):
        q_copy(d).wait_send()
    for p in range(seq):
        sib_copy(p, 0).wait_send()
        sib_copy(p, 1).wait_send()
        x_copy(p).wait_send()
        if p:
            out_copy(p).wait_send()
    for way in range(2):
        for t in range(seq - 1):
            for d in range(groups):

                @pl.when(can_send(way, t))
                def _():
                    att_copy(way, t, d, True).wait_send()


def fused(mesh, q_mant, q_exp, text_kv, out_weight, lengths):
    seq, n_head, n_sub = mesh.shape["seq"], mesh.shape["head"], mesh.shape["sub"]
    groups = n_head * n_sub
    rows = q_mant.shape[0]
    width, cols = out_weight.shape
    bf16 = jnp.bfloat16
    dma = pltpu.SemaphoreType.DMA
    return pl.pallas_call(
        functools.partial(kernel, (seq, n_head, n_sub, q_exp.shape[1])),
        out_shape=jax.ShapeDtypeStruct(q_mant.shape, bf16),
        in_specs=[
            pl.BlockSpec(memory_space=pltpu.VMEM),
            pl.BlockSpec(memory_space=pltpu.VMEM),
            pl.BlockSpec(memory_space=pltpu.SMEM),
            pl.BlockSpec(memory_space=pl.ANY),
            pl.BlockSpec(memory_space=pl.ANY),
        ],
        out_specs=pl.BlockSpec(memory_space=pltpu.VMEM),
        scratch_shapes=[
            pltpu.VMEM(text_kv.shape, bf16),
            pltpu.VMEM(out_weight.shape, bf16),
            pltpu.VMEM((groups, rows, width), bf16),
            pltpu.VMEM((groups, rows, width), bf16),
            pltpu.VMEM((seq, groups, rows, width), bf16),
            pltpu.VMEM((seq, groups, rows, cols), bf16),
            pltpu.VMEM((seq, n_head, rows, cols), bf16),
            pltpu.VMEM((seq, rows, cols), bf16),
            pltpu.VMEM((seq, rows, cols), bf16),
            pltpu.VMEM((seq, rows, cols), bf16),
            dma((3,)),
            dma((groups,)),
            dma((groups,)),
            dma((2, seq, groups)),
            dma((2, seq, groups)),
            dma((seq, 2)),
            dma((seq, 2)),
            dma((seq,)),
            dma((seq,)),
            dma((seq,)),
            dma((seq,)),
        ],
        compiler_params=pltpu.CompilerParams(
            collective_id=0, has_side_effects=True, vmem_limit_bytes=56 * 2**20
        ),
    )(q_mant, q_exp, lengths, text_kv, out_weight)


def fits(mesh, q_mant, q_exp, text_kv, out_weight, lengths):
    if (mesh.shape["seq"], mesh.shape["head"], mesh.shape["sub"]) != (4, 2, 2):
        return False
    head_size = q_mant.shape[1] // q_exp.shape[1]
    return (
        head_size == 128
        and q_mant.shape[0] * 4 == FRAME_TOK
        and q_mant.shape[0] % 16 == 0
        and (out_weight.shape[0] // head_size) % UNROLL == 0
        and out_weight.shape[1] % BLOCK == 0
    )


def shards(q_mant, q_exp, text_kv, out_weight, lengths):
    tok_dev = q_mant.shape[0]
    heads_all = q_exp.shape[1]
    groups = lax.axis_size("head") * lax.axis_size("sub")
    seq = lax.axis_size("seq")
    local_heads = heads_all // groups
    head_size = q_mant.shape[1] // heads_all
    rows = tok_dev * groups
    factor = jnp.exp2(q_exp.astype(jnp.float32))
    query = (
        q_mant.reshape(tok_dev, heads_all, head_size).astype(jnp.float32) * factor[:, :, None]
    ).astype(jnp.bfloat16)
    query = lax.all_to_all(
        query.reshape(q_mant.shape), ("head", "sub"), split_axis=1, concat_axis=0, tiled=True
    )
    query = query.reshape(rows, local_heads, head_size)
    keys = text_kv[0].reshape(-1, local_heads, head_size)
    values = text_kv[1].reshape(-1, local_heads, head_size)
    text_len = keys.shape[0]
    frames = lengths.shape[0]
    row_index = lax.axis_index("seq") * rows + jnp.arange(rows, dtype=jnp.int32)
    frame = row_index // FRAME_TOK
    limit = jnp.sum(
        jnp.where(
            frame[:, None] == jnp.arange(frames, dtype=jnp.int32)[None, :], lengths[None, :], 0
        ),
        axis=1,
    )
    valid = jnp.arange(text_len, dtype=jnp.int32)[None, :] < limit[:, None]
    scores = jnp.einsum("rhd,thd->hrt", query, keys, preferred_element_type=jnp.float32) * (
        1.0 / head_size**0.5
    )
    scores = jnp.where(valid[None], scores, -1e30)
    top = jnp.max(scores, axis=2, keepdims=True)
    probs = jnp.where(valid[None], jnp.exp(scores - top), 0.0)
    total = jnp.sum(probs, axis=2, keepdims=True)
    weights = (probs / total).astype(jnp.bfloat16)
    attended = jnp.einsum(
        "hrt,thd->rhd", weights, values, preferred_element_type=jnp.float32
    ).astype(jnp.bfloat16)
    attended = attended.reshape(rows, local_heads * head_size)
    gathered = lax.all_gather(attended, "seq", axis=0, tiled=False)
    term = jnp.dot(
        gathered.reshape(seq * rows, -1), out_weight, preferred_element_type=jnp.float32
    ).astype(jnp.bfloat16)
    cols = term.shape[1]
    term = term.reshape(seq, groups, tok_dev, cols).transpose(1, 0, 2, 3)
    summed = lax.psum_scatter(
        term.reshape(groups * seq * tok_dev, cols), ("head", "sub"), scatter_dimension=0, tiled=True
    )
    mixed = lax.all_to_all(
        summed.reshape(seq, tok_dev, cols), "seq", split_axis=0, concat_axis=0, tiled=True
    )
    return mixed.transpose(1, 0, 2).reshape(tok_dev, seq * cols)


def solution(mesh):
    def step(*arrays):
        return fused(mesh, *arrays) if fits(mesh, *arrays) else shards(*arrays)

    return jax.shard_map(
        step,
        mesh=mesh,
        in_specs=(
            P(("grp", "seq", "head", "sub"), None),
            P(("grp", "seq", "head", "sub"), None),
            P(None, "grp", ("head", "sub")),
            P(("head", "sub"), "seq"),
            P("grp"),
        ),
        out_specs=P(("grp", "seq", "head", "sub"), None),
        check_vma=False,
    )
```
